32 devices in a mesh: dp: 4 (over x, core), expert: 8 (over z, y).
Axes of the slice: x: 2, y: 2, z: 4, core: 2. Of those that a mesh axis runs over, the one named last changes fastest.
Arguments:
- tokens: bfloat16 [1024, 5120], P('expert', 'dp'), may hold values from -6 to 6
- out_grad: bfloat16 [1024, 5120], P('expert', 'dp'), may hold values from -0.59765625 to 0.59765625
- gate_values: float32 [1024, 2], P('expert'), may hold values from 0.05 to 0.5
- route_lists: int32 [1024, 2], P('expert'), may hold values from 0 to 3, all different within a row; in each aligned block of 128 rows (0 to 127, 128 to 255, ...) at most 72 rows name the same one
- expert_pairs: int32 [4], replicated, may hold values from 0 to 3, as said below
- gate_weight: bfloat16 [8, 5120, 1024], P('expert', 'dp'), as said below
- up_weight: bfloat16 [8, 5120, 1024], P('expert', 'dp'), as said below
- down_weight: bfloat16 [8, 1024, 5120], P('expert', None, 'dp'), as said below
Outputs:
- layer_output: bfloat16 [1024, 5120], P('expert', 'dp')
- token_grad: bfloat16 [1024, 5120], P('expert', 'dp')
- gate_value_grad: float32 [1024, 2], P('expert')
- gate_weight_grad: bfloat16 [8, 5120, 1024], P('expert', 'dp')
- up_weight_grad: bfloat16 [8, 5120, 1024], P('expert', 'dp')
- down_weight_grad: bfloat16 [8, 1024, 5120], P('expert', None, 'dp')
The draws below stay inside these ranges and needn't reach their ends.
Inputs may be any that keep to these rules, and one draw needn't show every extreme that they name: `route_lists`: each token names 2 different experts; within each aligned block of 128 tokens no expert is named by more than 72 tokens. `expert_pairs`: a permutation; pair p is made of slots p and p + 4. `gate_weight`: slots p and p + 4 hold equal matrices, those of expert expert_pairs[p]. `up_weight`: slots p and p + 4 hold equal matrices. `down_weight`: slots p and p + 4 hold equal matrices.
All inputs are finite; a program needn't handle non-finite values.
Results may differ from the reference program's by a relative error of at most 0.023.
Values may be sent and summed in bfloat16 or wider, within the bound.
No kernel may reach another device: no remote copies, remote signals or barrier semaphores. Data moves between devices by JAX's collectives and lax.ppermute only.
A program may use at most 128 MiB of HBM per device.

```python
import math
import jax
import jax.numpy as jnp
import numpy as np
from jax import lax

D = 5120
FF = 1024
TOK_DEV = 128
CAP = 72
HALF = 36
EXPERTS = 4
TOP = 2
TOKENS = 1024
N_DP = 4
N_EXPERT = 8


def pairing(key):
    return jax.random.permutation(jax.random.fold_in(key, 4242), EXPERTS).astype(jnp.int32)


def slot_matrices(key, salt, row_size, col_size, scale):
    order = pairing(key)
    slot_experts = order[jnp.arange(2 * EXPERTS, dtype=jnp.int32) % EXPERTS]
    base_key = jax.random.fold_in(key, salt)

    def one_slot(expert_id):
        slot_key = jax.random.fold_in(base_key, expert_id)
        values = jax.random.normal(slot_key, (row_size, col_size), jnp.float32)
        return values * scale
    return jax.vmap(one_slot)(slot_experts)


def draw_expert_pairs(key, part):
    return pairing(key)


def draw_gate_weight(key, part):
    return slot_matrices(key, 11, D, FF, D ** (-0.5)).astype(jnp.bfloat16)


def draw_up_weight(key, part):
    return slot_matrices(key, 12, D, FF, D ** (-0.5)).astype(jnp.bfloat16)


def draw_down_weight(key, part):
    return slot_matrices(key, 13, FF, D, FF ** (-0.5)).astype(jnp.bfloat16)


def steps_of(key, extent, shards, least, top_value):
    gain, own = 1.0, jax.random.fold_in(key, 6)
    for axis_at, parts in shards:
        heights = jnp.exp(jax.random.uniform(jax.random.fold_in(own, axis_at), (parts,), jnp.float32, least / len(shards), top_value / len(shards)))
        gain = gain * jnp.repeat(heights, extent[axis_at] // parts).reshape([-1 if axis == axis_at else 1 for axis in range(len(extent))])
    return gain


def routed_block(key, own, number, rows, number_of, top, reach, slope):
    order = jax.random.permutation(key, number_of)
    crowded, common = portions_of(number_of, rows * top, reach, slope, True), portions_of(number_of, rows * top, reach, slope, False)
    places = jnp.arange(number_of)

    def named(tallies, offset_by):
        used = int((tallies > 0).sum())
        fixed = max(1, used // 4)
        moved = fixed + (places - fixed + offset_by * (used - fixed)) % max(1, number_of - fixed)
        return jnp.zeros((number_of,), jnp.int32).at[order[jnp.where(places < fixed, places, moved)]].set(jnp.asarray(tallies, jnp.int32))

    tallies = jnp.where(number % 4 == 0, named(crowded, number // 4), named(common, number - number // 4 - 1))
    mixed = jax.random.permutation(jax.random.fold_in(own, 3), number_of)
    donor, taker = mixed[0:number_of // 2 * 2:2], mixed[1:number_of // 2 * 2:2]
    margin = jnp.minimum(tallies[donor] - 1, reach - tallies[taker]) // 2
    margin = jnp.where((donor == order[0]) | (taker == order[0]) | (tallies[taker] == 0), 0, jnp.maximum(margin, 0))
    moved = jax.random.randint(jax.random.fold_in(own, 4), (number_of // 2,), 0, 1 << 20) % (margin + 1)
    tallies = tallies.at[donor].add(-moved).at[taker].add(moved)
    labels = jnp.searchsorted(jnp.cumsum(tallies), jnp.arange(rows * top), side="right").astype(jnp.int32)
    grid = labels.reshape(top, rows).T
    grid = grid[jax.random.permutation(jax.random.fold_in(own, 1), rows)]
    offset_by = jax.random.randint(jax.random.fold_in(own, 2), (rows, 1), 0, top)
    return jnp.take_along_axis(grid, (jnp.arange(top)[None, :] + offset_by) % top, axis=1)


def portions_of(number_of, total, limit, slope, full):
    weights = [(1 << 20) // math.isqrt(grade ** slope) + 1 for grade in range(1, number_of + 1)]
    largest = limit if full else min(limit, max(-(-total // number_of), total * weights[0] // sum(weights)))
    least = 1 if total - largest >= number_of - 1 else 0
    holding, surplus = [largest] + [least] * (number_of - 1), total - largest - least * (number_of - 1)
    while surplus > 0:
        free = [i for i in range(1, number_of) if holding[i] < largest] or [i for i in range(1, number_of) if holding[i] < limit]
        whole, left = sum([weights[i] for i in free]), surplus
        for i in free:
            extra = min(limit - holding[i], max(1, left * weights[i] // whole), surplus)
            holding[i] = holding[i] + extra
            surplus = surplus - extra
    return np.array(holding)


def bell_draw(rng, shape, scale, bound, pieces=(), held_as=jnp.bfloat16):
    loudness = steps_of(rng, shape, pieces, -0.22, 0.18) if pieces else 1.0
    values = jax.random.normal(rng, shape, jnp.float32) * scale * loudness
    return jnp.minimum(jnp.maximum(values, -bound), bound).astype(held_as)


def setup_inputs(seed: int = 0) -> dict:
    seeds = jax.random.split(jax.random.key(seed), 9)
    tokens = bell_draw(seeds[0], (TOKENS, D), 1.0, 6.0, ((0, 8), (1, 4)))
    out_grad = bell_draw(seeds[1], (TOKENS, D), 0.1, 0.59765625, ((0, 8), (1, 4)))
    gate_values = jnp.clip(0.05 + 0.45 * jax.random.uniform(seeds[2], (TOKENS, TOP), jnp.float32) ** steps_of(seeds[2], (TOKENS, TOP), ((0, 8),), -0.2, 0.2), 0.05, 0.5)
    route_lists_keys = jax.random.split(jax.random.fold_in(seeds[3], 1), TOKENS // TOK_DEV)
    route_lists_turns = jax.random.permutation(jax.random.fold_in(seeds[3], 3), TOKENS // TOK_DEV)
    route_lists = jax.vmap(lambda own, number: routed_block(jax.random.fold_in(seeds[3], 2), own, number, TOK_DEV, EXPERTS, TOP, CAP, 2))(route_lists_keys, route_lists_turns).reshape((TOKENS, TOP))
    expert_pairs = draw_expert_pairs(jax.random.fold_in(seeds[8], 71), 0)
    gate_weight = draw_gate_weight(jax.random.fold_in(seeds[8], 71), 0)
    up_weight = draw_up_weight(jax.random.fold_in(seeds[8], 71), 0)
    down_weight = draw_down_weight(jax.random.fold_in(seeds[8], 71), 0)
    return {"tokens": tokens, "out_grad": out_grad, "gate_values": gate_values, "route_lists": route_lists, "expert_pairs": expert_pairs, "gate_weight": gate_weight, "up_weight": up_weight, "down_weight": down_weight}


def rounded(values):
    return lax.optimization_barrier(values.astype(jnp.bfloat16)).astype(jnp.float32)


def block_sums(rows_in, weight):
    width_dev = D // N_DP
    row_blocks = rows_in.astype(jnp.float32).reshape(rows_in.shape[0], N_DP, width_dev)
    weight_blocks = weight.astype(jnp.float32).reshape(N_DP, width_dev, weight.shape[1])
    partial_terms = jnp.einsum("rdk,dkf->rdf", row_blocks, weight_blocks)
    return jnp.sum(rounded(partial_terms), axis=1)


def back_block_sums(rows_in, weight):
    width_dev = D // N_DP
    row_blocks = rows_in.astype(jnp.float32).reshape(rows_in.shape[0], N_DP, width_dev)
    weight_blocks = weight.astype(jnp.float32).reshape(weight.shape[0], N_DP, width_dev)
    partial_terms = jnp.einsum("rdk,fdk->rdf", row_blocks, weight_blocks)
    return jnp.sum(rounded(partial_terms), axis=1)


def reference(tokens, out_grad, gate_values, route_lists, expert_pairs, gate_weight, up_weight, down_weight):
    catalog = jnp.arange(EXPERTS, dtype=jnp.int32)
    chosen = route_lists[:, :, None] == catalog[None, None, :]
    present = jnp.sum(chosen.astype(jnp.int32), axis=1)
    blocked = present.reshape(N_EXPERT, TOK_DEV, EXPERTS)
    before = (jnp.cumsum(blocked, axis=1) - blocked).reshape(TOKENS, EXPERTS)
    weight_sel = jnp.sum(jnp.where(chosen, gate_values[:, :, None], jnp.float32(0.0)), axis=1)
    block_id = jnp.arange(TOKENS, dtype=jnp.int32) // TOK_DEV
    pair_of = jnp.sum(jnp.where(expert_pairs[None, :] == catalog[:, None], catalog[None, :], 0), axis=1).astype(jnp.int32)
    row_total = N_EXPERT * CAP
    padded_tokens = jnp.concatenate([tokens, jnp.zeros((1, D), jnp.bfloat16)], axis=0)
    padded_grad = jnp.concatenate([out_grad.astype(jnp.float32), jnp.zeros((1, D), jnp.float32)], axis=0)
    first_half = (jnp.arange(row_total, dtype=jnp.int32) % CAP) < HALF

    def halves(left, right):
        first_rows = jnp.where(first_half[:, None], left, jnp.zeros_like(left))
        other_rows = jnp.where(first_half[:, None], jnp.zeros_like(left), left)
        first_part = rounded(jnp.dot(first_rows.T, right, preferred_element_type=jnp.float32))
        other_part = rounded(jnp.dot(other_rows.T, right, preferred_element_type=jnp.float32))
        return (first_part + other_part).astype(jnp.bfloat16)

    def per_expert(state_now, expert_id):
        output_acc, grad_acc, inner_dots = state_now
        dest_row = jnp.where(present[:, expert_id] > 0, block_id * CAP + before[:, expert_id], row_total).astype(jnp.int32)
        slot_table = jnp.full((row_total + 1,), TOKENS, jnp.int32).at[dest_row].set(jnp.arange(TOKENS, dtype=jnp.int32))[:row_total]
        rows_in = padded_tokens[slot_table]
        padded_weight = jnp.concatenate([weight_sel[:, expert_id], jnp.zeros((1,), jnp.float32)], axis=0)
        row_weight = padded_weight[slot_table]
        grad_rows = padded_grad[slot_table]
        cot_rows = (row_weight[:, None] * grad_rows).astype(jnp.bfloat16)
        pair_index = pair_of[expert_id]
        w_gate = gate_weight[pair_index]
        w_up = up_weight[pair_index]
        w_down = down_weight[pair_index]
        gate_pre = block_sums(rows_in, w_gate)
        up_pre = block_sums(rows_in, w_up)
        hidden = (jax.nn.silu(gate_pre) * up_pre).astype(jnp.bfloat16)
        expert_out = jnp.dot(hidden, w_down, preferred_element_type=jnp.float32).astype(jnp.bfloat16)
        hidden_grad = back_block_sums(cot_rows, w_down)
        sigmoid_gate = jax.nn.sigmoid(gate_pre)
        up_grad = (hidden_grad * gate_pre * sigmoid_gate).astype(jnp.bfloat16)
        pre_grad = (hidden_grad * up_pre * sigmoid_gate * (1.0 + gate_pre * (1.0 - sigmoid_gate))).astype(jnp.bfloat16)
        row_input_grad = (jnp.dot(pre_grad, w_gate.T, preferred_element_type=jnp.float32) + jnp.dot(up_grad, w_up.T, preferred_element_type=jnp.float32)).astype(jnp.bfloat16)
        grad_gate = halves(rows_in, pre_grad)
        grad_up = halves(rows_in, up_grad)
        grad_down = halves(hidden, cot_rows)
        out_float = expert_out.astype(jnp.float32)
        output_acc = output_acc.at[slot_table].add(row_weight[:, None] * out_float)
        grad_acc = grad_acc.at[slot_table].add(row_input_grad.astype(jnp.float32))
        inner_dots = inner_dots.at[slot_table, expert_id].set(jnp.sum(grad_rows * out_float, axis=1))
        return (output_acc, grad_acc, inner_dots), (grad_gate, grad_up, grad_down)

    start_state = (jnp.zeros((TOKENS + 1, D), jnp.float32), jnp.zeros((TOKENS + 1, D), jnp.float32), jnp.zeros((TOKENS + 1, EXPERTS), jnp.float32))
    final_state, expert_grads = lax.scan(per_expert, start_state, catalog)
    output_acc, grad_acc, inner_dots = final_state
    layer_output = output_acc[:TOKENS].astype(jnp.bfloat16)
    token_grad = grad_acc[:TOKENS].astype(jnp.bfloat16)
    gate_value_grad = jnp.take_along_axis(inner_dots[:TOKENS], route_lists, axis=1)
    slot_experts = expert_pairs[jnp.arange(2 * EXPERTS, dtype=jnp.int32) % EXPERTS]
    gate_weight_grad = expert_grads[0][slot_experts]
    up_weight_grad = expert_grads[1][slot_experts]
    down_weight_grad = expert_grads[2][slot_experts]
    return (layer_output, token_grad, gate_value_grad, gate_weight_grad, up_weight_grad, down_weight_grad)
```

```python
import jax
import jax.numpy as jnp
from jax import lax
from jax.sharding import PartitionSpec as P

HALF = 36
CAP = 2 * HALF
FIRST = (((0,), (0,)), ((), ()))
SECOND = (((1,), (1,)), ((), ()))


def hop(x, axis, distance):
    return lax.ppermute(x, axis, [(i, i ^ distance) for i in range(lax.axis_size(axis))])


def dot32(a, b, dims=(((1,), (0,)), ((), ()))):
    return lax.dot_general(a, b, dims, preferred_element_type=jnp.float32)


def routing(routes, gates, names):
    tok = routes.shape[1]
    hits = routes[:, None, :] == names[None, :, None]
    named = jnp.any(hits, axis=0)
    earlier = jnp.arange(tok)[:, None] < jnp.arange(tok)[None, :]
    before = dot32(named.astype(jnp.bfloat16), earlier.astype(jnp.bfloat16)).astype(jnp.int32)
    place = jnp.where(named, before, -1)
    pick = place[:, None, :] == jnp.arange(CAP)[None, :, None]
    gate_at = jnp.sum(jnp.where(hits, gates[:, None, :], 0.0), axis=0)
    row_gate = jnp.sum(jnp.where(pick, gate_at[:, None, :], 0.0), axis=2)
    return hits, pick, row_gate.reshape(-1)


def dispatch(pick, block, scale=None):
    rows = dot32(pick.reshape(-1, pick.shape[2]).astype(jnp.bfloat16), block)
    if scale is not None:
        rows = rows * scale[:, None]
    rows = rows.astype(jnp.bfloat16)
    parts = [rows[:CAP]]
    for d in range(1, pick.shape[0]):
        parts.append(hop(rows[d * CAP : (d + 1) * CAP], "expert", d))
    return jnp.concatenate(parts, axis=0)


def forward(rows, cot, w_gate, w_up, w_down, core):
    width = w_gate.shape[1] // 2
    parts = [dot32(rows, w_gate), dot32(rows, w_up), dot32(cot, w_down, SECOND)]
    parts = [p.astype(jnp.bfloat16) for p in parts]

    def side(which):
        return jnp.concatenate(
            [lax.dynamic_slice_in_dim(p, which * width, width, axis=1) for p in parts], axis=1
        )

    total = side(core).astype(jnp.float32) + hop(side(1 - core), "dp", 1).astype(jnp.float32)
    total = total.astype(jnp.bfloat16)
    distance = 2
    while distance < lax.axis_size("dp"):
        total = total.astype(jnp.float32) + hop(total, "dp", distance).astype(jnp.float32)
        total = total.astype(jnp.bfloat16)
        distance *= 2
    other = hop(total, "dp", 1)
    low = jnp.where(core == 0, total, other).astype(jnp.float32)
    high = jnp.where(core == 0, other, total).astype(jnp.float32)
    return [
        jnp.concatenate([low[:, i * width : (i + 1) * width], high[:, i * width : (i + 1) * width]], axis=1)
        for i in range(3)
    ]


def middle(gate_pre, up_pre, hidden_grad):
    sig = jax.nn.sigmoid(gate_pre)
    silu = gate_pre * sig
    hidden = (silu * up_pre).astype(jnp.bfloat16)
    up_grad = (hidden_grad * silu).astype(jnp.bfloat16)
    pre_grad = (hidden_grad * up_pre * sig * (1.0 + gate_pre * (1.0 - sig))).astype(jnp.bfloat16)
    return hidden, up_grad, pre_grad


def shards(
    tokens, out_grad, gate_values, route_lists, expert_pairs, gate_weight, up_weight, down_weight
):
    top = route_lists.shape[1]
    width = tokens.shape[1]
    pairs = lax.axis_size("expert") // 2
    low = lax.axis_index("expert") % pairs
    core = lax.axis_index("dp") % 2
    places = jnp.arange(pairs, dtype=jnp.int32)
    names = jnp.sum(
        jnp.where((low ^ places)[:, None] == places[None, :], expert_pairs[None, :], 0), axis=1
    )
    w_gate, w_up, w_down = gate_weight[0], up_weight[0], down_weight[0]

    routes, gates = route_lists.T, gate_values.T
    info = jnp.concatenate([routes.astype(jnp.float32), gates], axis=0)
    far_info = hop(info, "expert", pairs)
    hits, pick, row_gate = routing(routes, gates, names)
    rows = dispatch(pick, tokens)
    far_tokens = hop(tokens, "expert", pairs)
    cot = dispatch(pick, out_grad, row_gate)
    far_grad = hop(out_grad, "expert", pairs)

    gate_pre, up_pre, hidden_grad = forward(rows, cot, w_gate, w_up, w_down, core)
    hidden, up_grad, pre_grad = middle(gate_pre, up_pre, hidden_grad)
    inner = jnp.sum(hidden.astype(jnp.float32) * hidden_grad, axis=1, keepdims=True)
    inner_high = inner.astype(jnp.bfloat16)
    inner_low = (inner - inner_high.astype(jnp.float32)).astype(jnp.bfloat16)

    expert_out = dot32(hidden, w_down).astype(jnp.bfloat16)
    input_grad = (dot32(pre_grad, w_gate, SECOND) + dot32(up_grad, w_up, SECOND)).astype(
        jnp.bfloat16
    )
    back = jnp.concatenate(
        [expert_out, input_grad, jnp.pad(jnp.concatenate([inner_high, inner_low], axis=1), ((0, 0), (0, 126)))],
        axis=1,
    )
    back = jnp.concatenate(
        [back[:CAP]] + [hop(back[d * CAP : (d + 1) * CAP], "expert", d) for d in range(1, pairs)],
        axis=0,
    )
    all_pick = pick.reshape(pairs * CAP, -1).astype(jnp.bfloat16)
    token_grad = dot32(all_pick, back[:, width : 2 * width], FIRST).astype(jnp.bfloat16)
    layer_output = 0.0
    inners = []
    for k in range(top):
        mine = (pick & hits[k][:, None, :]).reshape(pairs * CAP, -1).astype(jnp.bfloat16)
        layer_output += gate_values[:, k : k + 1] * dot32(mine, back[:, :width], FIRST)
        ends = dot32(mine, back[:, 2 * width :], FIRST)
        inners.append(ends[:, 0:1] + ends[:, 1:2])
    layer_output = layer_output.astype(jnp.bfloat16)
    gate_value_grad = jnp.concatenate(inners, axis=1) / gate_values

    far_routes, far_gates = far_info[:top].astype(jnp.int32), far_info[top:]
    _, far_pick, far_row_gate = routing(far_routes, far_gates, names)
    far_rows = dispatch(far_pick, far_tokens)
    far_cot = dispatch(far_pick, far_grad, far_row_gate)
    far_hidden, far_up, far_pre = middle(*forward(far_rows, far_cot, w_gate, w_up, w_down, core))

    def both(a, b):
        return jnp.concatenate([a, b], axis=0)

    all_rows = both(rows, far_rows)
    grad_gate = dot32(all_rows, both(pre_grad, far_pre), FIRST).astype(jnp.bfloat16)
    grad_up = dot32(all_rows, both(up_grad, far_up), FIRST).astype(jnp.bfloat16)
    grad_down = dot32(both(hidden, far_hidden), both(cot, far_cot), FIRST).astype(jnp.bfloat16)
    return layer_output, token_grad, gate_value_grad, grad_gate[None], grad_up[None], grad_down[None]


def solution(mesh):
    row = P("expert", "dp")
    small = P("expert", None)
    tall = P("expert", "dp", None)
    wide = P("expert", None, "dp")
    return jax.shard_map(
        shards,
        mesh=mesh,
        in_specs=(row, row, small, small, P(), tall, tall, wide),
        out_specs=(row, row, small, tall, tall, wide),
        check_vma=False,
    )
```

```python
import functools

import jax
import jax.numpy as jnp
from jax import lax
from jax.experimental import pallas as pl
from jax.experimental.pallas import tpu as pltpu
from jax.sharding import PartitionSpec as P

HALF = 36
CAP = 2 * HALF
EXTRA = 128
BLOCK = 32
FIRST = (((0,), (0,)), ((), ()))
SECOND = (((1,), (1,)), ((), ()))
PLAIN = (((1,), (0,)), ((), ()))
F32 = jnp.float32
BF16 = jnp.bfloat16

VMEM = pl.BlockSpec(memory_space=pltpu.VMEM)
SMEM = pl.BlockSpec(memory_space=pltpu.SMEM)
ANY = pl.BlockSpec(memory_space=pl.ANY)


def hop(x, axis, distance):
    return lax.ppermute(x, axis, [(i, i ^ distance) for i in range(lax.axis_size(axis))])


def after(x, *first):
    return lax.optimization_barrier((x, *first))[0]


def dot32(a, b, dims=PLAIN):
    return lax.dot_general(a, b, dims, preferred_element_type=F32)


def struct(shape, dtype=BF16):
    return jax.ShapeDtypeStruct(shape, dtype)


def call(kernel, name, out_shape, in_specs, out_specs, scratch=(), mib=20):
    return pl.pallas_call(
        kernel,
        out_shape=out_shape,
        in_specs=in_specs,
        out_specs=out_specs,
        scratch_shapes=scratch,
        compiler_params=pltpu.CompilerParams(vmem_limit_bytes=mib * 2**20),
        cost_estimate=pl.CostEstimate(flops=1024, bytes_accessed=1 << 19, transcendentals=0),
        name=name,
    )


def row_slots(pairs_ref):
    pairs = pairs_ref.shape[0]
    low = lax.axis_index("expert") % pairs
    at = lax.broadcasted_iota(jnp.int32, (pairs * CAP, 1), 0)
    name = jnp.full(at.shape, pairs_ref[low], jnp.int32)
    place = at
    for d in range(1, pairs):
        later = at >= d * CAP
        name = jnp.where(later, pairs_ref[low ^ d], name)
        place = jnp.where(later, at - d * CAP, place)
    return name.astype(F32), place.astype(F32)


def pick_rows(routes, gates, pairs_ref):
    top, tok = routes.shape
    name, place = row_slots(pairs_ref)
    gate = jnp.zeros((name.shape[0], tok), F32)
    named = jnp.zeros((name.shape[0], tok), F32)
    hits = [routes[k : k + 1] == name for k in range(top)]
    for k in range(top):
        named = jnp.where(hits[k], 1.0, named)
        gate = jnp.where(hits[k], gates[k : k + 1], gate)
    earlier = (
        lax.broadcasted_iota(jnp.int32, (tok, tok), 0) < lax.broadcasted_iota(jnp.int32, (tok, tok), 1)
    )
    before = dot32(named.astype(BF16), jnp.where(earlier, 1.0, 0.0).astype(BF16))
    return jnp.where(before == place, named, 0.0), gate, hits


def put_chunks(rows, refs):
    for d, ref in enumerate(refs):
        ref[...] = rows[d * CAP : (d + 1) * CAP].astype(BF16)


def join(refs):
    return jnp.concatenate([r[...].astype(F32) for r in refs], axis=0).astype(BF16)


def pack_own_kernel(pairs, pairs_ref, routes_ref, gates_ref, tok_ref, grad_ref, far_ref, *outs):
    top, tok = routes_ref.shape
    width = tok_ref.shape[1]
    routes = routes_ref[...].astype(F32)
    gates = gates_ref[...]
    far_ref[:, :width] = tok_ref[...]
    high = gates.astype(BF16).astype(F32)
    mid = (gates - high).astype(BF16).astype(F32)
    filler = jnp.zeros((EXTRA - 4 * top, tok), F32)
    info = jnp.concatenate([routes, high, mid, gates - high - mid, filler], axis=0)
    far_ref[:, width:] = info.T.astype(BF16)
    pick, gate, _ = pick_rows(routes, gates, pairs_ref)
    row_gate = jnp.sum(pick * gate, axis=1, keepdims=True)
    pick = pick.astype(BF16)
    put_chunks(dot32(pick, tok_ref[...]), [ref.at[:, :width] for ref in outs])
    put_chunks(dot32(pick, grad_ref[...]) * row_gate, [ref.at[:, width:] for ref in outs])


def pack_own(expert_pairs, routes, gates, tokens, out_grad):
    tok, width = tokens.shape
    pairs = expert_pairs.shape[0]
    out = call(
        functools.partial(pack_own_kernel, pairs),
        "pack_own",
        [struct((tok, width + EXTRA))] + [struct((CAP, 2 * width))] * pairs,
        [SMEM] + [VMEM] * 4,
        [VMEM] * (1 + pairs),
        mib=PACK_MIB,
    )(expert_pairs, routes, gates, tokens, out_grad)
    return out[0], list(out[1:])


PACK_MIB = 56


def pack_far_kernel(top, pairs_ref, far_ref, grad_ref, *outs):
    width = grad_ref.shape[1]
    info = far_ref[:, width:].astype(F32).T
    gates = info[top : 2 * top] + info[2 * top : 3 * top] + info[3 * top : 4 * top]
    pick, gate, _ = pick_rows(info[:top], gates, pairs_ref)
    row_gate = jnp.sum(pick * gate, axis=1, keepdims=True)
    pick = pick.astype(BF16)
    put_chunks(dot32(pick, far_ref[:, :width]), [ref.at[:, :width] for ref in outs])
    put_chunks(dot32(pick, grad_ref[...]) * row_gate, [ref.at[:, width:] for ref in outs])


def pack_far(expert_pairs, far, out_grad, top):
    pairs = expert_pairs.shape[0]
    out = call(
        functools.partial(pack_far_kernel, top),
        "pack_far",
        [struct((CAP, 2 * out_grad.shape[1]))] * pairs,
        [SMEM, VMEM, VMEM],
        [VMEM] * pairs,
    )(expert_pairs, far, out_grad)
    return list(out)


def dispatch(chunks, ordered=True):
    pairs = len(chunks)
    split = pairs - pairs // 4 if ordered else pairs
    near = [chunks[0]] + [hop(chunks[d], "expert", d) for d in range(1, split)]
    rest = [hop(after(chunks[d], *near[1:]), "expert", d) for d in range(split, pairs)]
    return near + rest


def load_kernel(*refs):
    copies = [pltpu.make_async_copy(refs[i], refs[3 + i], refs[6].at[i]) for i in range(3)]
    for copy in copies:
        copy.start()
    for copy in copies:
        copy.wait()


def load(weights):
    return call(
        load_kernel,
        "load",
        [struct(w.shape) for w in weights],
        [ANY] * 3,
        [VMEM] * 3,
        [pltpu.SemaphoreType.DMA((3,))],
    )(*weights)


def terms_kernel(count, *refs):
    chunks, (w_gate, w_up, w_down, rows_ref, cot_ref, send_ref, keep_ref) = refs[:count], refs[count:]
    half = send_ref.shape[2]
    width = rows_ref.shape[1]
    core = lax.axis_index("dp") % 2
    rows_ref[...] = join([ref.at[:, :width] for ref in chunks])
    cot_ref[...] = join([ref.at[:, width:] for ref in chunks])
    for ref, side in ((send_ref, 1 - core), (keep_ref, core)):
        at = pl.ds(pl.multiple_of(side * half, half), half)
        ref[0] = dot32(rows_ref[...], w_gate[:, at]).astype(BF16)
        ref[1] = dot32(rows_ref[...], w_up[:, at]).astype(BF16)
        ref[2] = dot32(cot_ref[...], w_down[at, :], SECOND).astype(BF16)


def terms(chunks, weights):
    total, width = len(chunks) * CAP, chunks[0].shape[1] // 2
    out = struct((3, total, weights[0].shape[1] // 2))
    return call(
        functools.partial(terms_kernel, len(chunks)),
        "terms",
        [struct((total, width))] * 2 + [out, out],
        [VMEM] * (len(chunks) + 3),
        [VMEM] * 4,
    )(*chunks, *weights)


def add_kernel(*refs):
    *parts, out = refs
    for i in range(out.shape[0]):
        sums = [a[i].astype(F32) + b[i].astype(F32) for a, b in zip(parts[::2], parts[1::2])]
        out[i] = jnp.concatenate(sums, axis=0).astype(BF16)


def add(*arrays):
    total = sum(a.shape[1] for a in arrays[::2])
    shape = arrays[0].shape
    return call(
        add_kernel, "add", struct((shape[0], total, shape[2])), [VMEM] * len(arrays), VMEM
    )(*arrays)


def core_hop(x):
    return hop(x, "dp", 1)


def across(total):
    distance = 2
    parts = [total, hop(total, "dp", distance)]
    while 2 * distance < lax.axis_size("dp"):
        distance *= 2
        total = add(*parts)
        parts = [total, hop(total, "dp", distance)]
    return parts


def middle(gate_pre, up_pre, hidden_grad):
    sig = jax.nn.sigmoid(gate_pre)
    silu = gate_pre * sig
    hidden = silu * up_pre
    up_grad = hidden_grad * silu
    pre_grad = hidden_grad * up_pre * sig * (1.0 + gate_pre * (1.0 - sig))
    return hidden, up_grad, pre_grad


def by_blocks(total, body):
    block = BLOCK if total % BLOCK == 0 else 16

    def step(i, carry):
        body(pl.ds(pl.multiple_of(i * block, block), block))
        return carry

    lax.fori_loop(0, total // block, step, 0)


def sides(mine, other):
    lower = lax.axis_index("dp") % 2 == 0

    def read(side, i, rows):
        a, b = mine[i, rows].astype(F32), other[i, rows].astype(F32)
        return jnp.where(lower, a, b) if side == 0 else jnp.where(lower, b, a)

    return read


def outputs_kernel(pairs, mine, other, w_gate, w_up, w_down, hidden_ref, up_ref, pre_ref, *refs):
    chunks, ends = refs[:pairs], refs[pairs]
    total, half = mine.shape[1:]
    width = w_gate.shape[0]
    read = sides(mine, other)

    def block(rows):
        inner = 0.0
        for side in range(2):
            values = [read(side, i, rows) for i in range(3)]
            hidden, up_grad, pre_grad = middle(*values)
            inner += jnp.sum(hidden * values[2], axis=1, keepdims=True)
            at = slice(side * half, (side + 1) * half)
            hidden_ref[rows, at] = hidden.astype(BF16)
            up_ref[rows, at] = up_grad.astype(BF16)
            pre_ref[rows, at] = pre_grad.astype(BF16)
        high = inner.astype(BF16).astype(F32)
        lane = lax.broadcasted_iota(jnp.int32, (inner.shape[0], EXTRA), 1)
        ends[rows] = jnp.where(lane == 0, high, jnp.where(lane == 1, inner - high, 0.0))

    by_blocks(total, block)
    put_chunks(ends[...], [ref.at[:, 2 * width :] for ref in chunks])
    out = dot32(hidden_ref[...], w_down[...])
    put_chunks(out, [ref.at[:, :width] for ref in chunks])
    out = dot32(pre_ref[...], w_gate[...], SECOND) + dot32(up_ref[...], w_up[...], SECOND)
    put_chunks(out, [ref.at[:, width : 2 * width] for ref in chunks])


def outputs(mine, other, weights, pairs):
    width, hidden = weights[0].shape
    total = pairs * CAP
    out = call(
        functools.partial(outputs_kernel, pairs),
        "outputs",
        [struct((total, hidden))] * 3 + [struct((CAP, 2 * width + EXTRA))] * pairs,
        [VMEM] * 5,
        [VMEM] * (3 + pairs),
        [pltpu.VMEM((total, EXTRA), F32)],
    )(mine, other, *weights)
    return out[:3], list(out[3:])


def combine_kernel(pairs, pairs_ref, routes_ref, gates_ref, *refs):
    chunks = refs[:pairs]
    out_ref, grad_ref, value_ref, back = refs[pairs:]
    tok, width = out_ref.shape
    top = routes_ref.shape[0]
    gates = gates_ref[...]
    pick, gate, hits = pick_rows(routes_ref[...].astype(F32), gates, pairs_ref)
    back[...] = join(chunks)
    scaled = pick * gate
    high = scaled.astype(BF16).astype(F32)
    both = jnp.concatenate([high, scaled - high], axis=1).astype(BF16)
    out = dot32(both, back[:, :width], FIRST)
    out_ref[...] = (out[:tok] + out[tok:]).astype(BF16)
    grad_ref[...] = dot32(pick.astype(BF16), back[:, width : 2 * width], FIRST).astype(BF16)
    ends = back[:, 2 * width :].astype(F32)
    inner = ends[:, 0:1] + ends[:, 1:2]
    values = [jnp.sum(jnp.where(hit, pick * inner, 0.0), axis=0, keepdims=True) for hit in hits]
    value_ref[...] = jnp.concatenate(values, axis=0) / gates


def combine(expert_pairs, routes, gates, chunks, width):
    top, tok = routes.shape
    pairs = len(chunks)
    return call(
        functools.partial(combine_kernel, pairs),
        "combine",
        [struct((tok, width)), struct((tok, width)), struct((top, tok), F32)],
        [SMEM] + [VMEM] * (2 + pairs),
        [VMEM] * 3,
        [pltpu.VMEM((pairs * CAP, chunks[0].shape[1]), BF16)],
    )(expert_pairs, routes, gates, *chunks)


def turn_kernel(*refs):
    *parts, out = refs
    out[...] = join(parts).T


def turn(parts):
    shape = (parts[0].shape[1], sum(p.shape[0] for p in parts))
    return call(turn_kernel, "turn", struct(shape), [VMEM] * len(parts), VMEM)(*parts)


def column_step(*widths):
    step = 256
    while any(w % step for w in widths):
        step //= 2
    return step


def grad_shapes(width, units):
    return [struct(shape) for shape in ((width, units), (width, units), (units, width))]


def own_grads_kernel(step, turned, pre_grad, up_grad, hidden, *refs):
    *cots, gate_out, up_out, down_out, cot = refs
    cot[...] = join(cots)
    for left, right, out in (
        (turned[...], pre_grad, gate_out),
        (turned[...], up_grad, up_out),
        (hidden[...].T, cot, down_out),
    ):
        for j in range(out.shape[1] // step):
            at = slice(j * step, (j + 1) * step)
            out[:, at] = dot32(left, right[:, at]).astype(BF16)


def own_grads(turned, pre_grad, up_grad, hidden, cots):
    width, total = turned.shape
    units = hidden.shape[1]
    return call(
        functools.partial(own_grads_kernel, column_step(units, width)),
        "own_grads",
        grad_shapes(width, units),
        [VMEM] * (4 + len(cots)),
        [VMEM] * 3,
        [pltpu.VMEM((total, width), BF16)],
    )(turned, pre_grad, up_grad, hidden, *cots)


def grads_kernel(step, mine, other, turned, cot, *refs):
    partial, outs, held, buffers, sems = refs[:3], refs[3:6], refs[6], refs[7:10], refs[10]
    total, half = mine.shape[1:]
    read = sides(mine, other)

    def block(rows):
        for side in range(2):
            far_hidden, up, pre = middle(*(read(side, i, rows) for i in range(3)))
            at = slice(side * half, (side + 1) * half)
            for i, part in enumerate((pre, up, far_hidden)):
                held[i, rows, at] = part.astype(BF16)

    by_blocks(total, block)
    copies = []
    for i, right in enumerate((held.at[0], held.at[1], cot)):
        left = held[2].T if i == 2 else turned[...]
        for j in range(outs[i].shape[1] // step):
            at = slice(j * step, (j + 1) * step)
            part = dot32(left, right[:, at]) + partial[i][:, at].astype(F32)
            buffers[i][:, at] = part.astype(BF16)
            copy = pltpu.make_async_copy(buffers[i].at[:, at], outs[i].at[:, at], sems.at[len(copies)])
            copy.start()
            copies.append(copy)
    for copy in copies:
        copy.wait()


def grads(mine, other, turned, cot, partial):
    width, total = turned.shape
    units = partial[0].shape[1]
    step = column_step(units, width)
    shapes = grad_shapes(width, units)
    return call(
        functools.partial(grads_kernel, step),
        "grads",
        shapes,
        [VMEM] * 7,
        [ANY] * 3,
        [pltpu.VMEM((3, total, units), BF16)]
        + [pltpu.VMEM(shape.shape, BF16) for shape in shapes]
        + [pltpu.SemaphoreType.DMA((2 * units // step + width // step,))],
        mib=24,
    )(mine, other, turned, cot, *partial)


def shards(
    tokens, out_grad, gate_values, route_lists, expert_pairs, gate_weight, up_weight, down_weight
):
    top = route_lists.shape[1]
    width = tokens.shape[1]
    pairs = lax.axis_size("expert") // 2
    routes, gates = route_lists.T, gate_values.T

    far, chunks = pack_own(expert_pairs, routes, gates, tokens, out_grad)
    weights = load([after(gate_weight[0], far), up_weight[0], down_weight[0]])
    far = hop(far, "expert", pairs)
    far_grad = hop(after(out_grad, far), "expert", pairs)
    chunks = dispatch(chunks)

    rows_a, cot_a, send, keep = terms(chunks[:1], weights)
    sums_a = across(add(keep, core_hop(send)))

    far_chunks = pack_far(expert_pairs, far, after(far_grad, sums_a[1]), top)
    chunks[1] = after(chunks[1], far_chunks[0])
    rows_b, cot_b, send, keep = terms(chunks[1:], weights)
    far_chunks = dispatch(far_chunks)
    sums_b = across(add(keep, core_hop(send)))

    far_chunks[1] = after(far_chunks[1], sums_b[1])
    mine = add(*sums_a, *sums_b)
    other = core_hop(mine)
    far_chunks[2] = after(far_chunks[2], mine)
    far_rows, far_cot, send, keep = terms(far_chunks, weights)
    got = core_hop(send)
    (hidden, up_grad, pre_grad), sent = outputs(after(mine, send), other, weights, pairs)
    far_sums = across(add(keep, after(got, sent[0])))
    arrived = dispatch(sent, False)
    turned = turn([after(rows_a, far_sums[0]), rows_b])
    far_turned = turn([after(far_rows, turned)])
    partial = own_grads(turned, pre_grad, up_grad, hidden, [cot_a, cot_b])

    far_sums[1] = after(far_sums[1], far_turned, *partial, *arrived)
    mine = add(*far_sums)
    other = core_hop(mine)
    layer_output, token_grad, values = combine(
        expert_pairs, routes, gates, [after(arrived[0], mine)] + arrived[1:], width
    )
    grad_gate, grad_up, grad_down = grads(
        mine, after(other, token_grad), far_turned, far_cot, partial
    )
    return layer_output, token_grad, values.T, grad_gate[None], grad_up[None], grad_down[None]


def solution(mesh):
    row = P("expert", "dp")
    small = P("expert", None)
    tall = P("expert", "dp", None)
    wide = P("expert", None, "dp")
    return jax.shard_map(
        shards,
        mesh=mesh,
        in_specs=(row, row, small, small, P(), tall, tall, wide),
        out_specs=(row, row, small, tall, tall, wide),
        check_vma=False,
    )
```

```python
import functools

import jax
import jax.numpy as jnp
from jax import lax
from jax.experimental import pallas as pl
from jax.experimental.pallas import tpu as pltpu
from jax.sharding import PartitionSpec as P

HALF = 36
CAP = 2 * HALF
EXTRA = 128
BLOCK = 96
FIRST = (((0,), (0,)), ((), ()))
SECOND = (((1,), (1,)), ((), ()))
PLAIN = (((1,), (0,)), ((), ()))
F32 = jnp.float32
BF16 = jnp.bfloat16

VMEM = pl.BlockSpec(memory_space=pltpu.VMEM)
SMEM = pl.BlockSpec(memory_space=pltpu.SMEM)
ANY = pl.BlockSpec(memory_space=pl.ANY)


def hop(x, axis, distance):
    return lax.ppermute(x, axis, [(i, i ^ distance) for i in range(lax.axis_size(axis))])


def after(x, *first):
    return lax.optimization_barrier((x, *first))[0]


def dot32(a, b, dims=PLAIN):
    return lax.dot_general(a, b, dims, preferred_element_type=F32)


def struct(shape, dtype=BF16):
    return jax.ShapeDtypeStruct(shape, dtype)


def call(kernel, name, out_shape, in_specs, out_specs, scratch=(), mib=20):
    return pl.pallas_call(
        kernel,
        out_shape=out_shape,
        in_specs=in_specs,
        out_specs=out_specs,
        scratch_shapes=scratch,
        compiler_params=pltpu.CompilerParams(vmem_limit_bytes=mib * 2**20),
        cost_estimate=pl.CostEstimate(flops=1024, bytes_accessed=1 << 19, transcendentals=0),
        name=name,
    )


def row_slots(pairs_ref):
    pairs = pairs_ref.shape[0]
    low = lax.axis_index("expert") % pairs
    at = lax.broadcasted_iota(jnp.int32, (pairs * CAP, 1), 0)
    name = jnp.full(at.shape, pairs_ref[low], jnp.int32)
    place = at
    for d in range(1, pairs):
        later = at >= d * CAP
        name = jnp.where(later, pairs_ref[low ^ d], name)
        place = jnp.where(later, at - d * CAP, place)
    return name.astype(F32), place.astype(F32)


def pick_rows(routes, gates, pairs_ref):
    top, tok = routes.shape
    name, place = row_slots(pairs_ref)
    gate = jnp.zeros((name.shape[0], tok), F32)
    named = jnp.zeros((name.shape[0], tok), F32)
    hits = [routes[k : k + 1] == name for k in range(top)]
    for k in range(top):
        named = jnp.where(hits[k], 1.0, named)
        gate = jnp.where(hits[k], gates[k : k + 1], gate)
    earlier = (
        lax.broadcasted_iota(jnp.int32, (tok, tok), 0) < lax.broadcasted_iota(jnp.int32, (tok, tok), 1)
    )
    before = dot32(named.astype(BF16), jnp.where(earlier, 1.0, 0.0).astype(BF16))
    return jnp.where(before == place, named, 0.0), gate, hits


def put_chunks(rows, refs):
    for d, ref in enumerate(refs):
        ref[...] = rows[d * CAP : (d + 1) * CAP].astype(BF16)


def join(refs):
    return jnp.concatenate([r[...].astype(F32) for r in refs], axis=0).astype(BF16)


def pack_own_kernel(pairs, pairs_ref, routes_ref, gates_ref, tok_ref, grad_ref, far_ref, *outs):
    top, tok = routes_ref.shape
    width = tok_ref.shape[1]
    routes = routes_ref[...].astype(F32)
    gates = gates_ref[...]
    far_ref[:, :width] = tok_ref[...]
    high = gates.astype(BF16).astype(F32)
    mid = (gates - high).astype(BF16).astype(F32)
    filler = jnp.zeros((EXTRA - 4 * top, tok), F32)
    info = jnp.concatenate([routes, high, mid, gates - high - mid, filler], axis=0)
    far_ref[:, width:] = info.T.astype(BF16)
    pick, gate, _ = pick_rows(routes, gates, pairs_ref)
    row_gate = jnp.sum(pick * gate, axis=1, keepdims=True)
    pick = pick.astype(BF16)
    put_chunks(dot32(pick, tok_ref[...]), [ref.at[:, :width] for ref in outs])
    put_chunks(dot32(pick, grad_ref[...]) * row_gate, [ref.at[:, width:] for ref in outs])


def pack_own(expert_pairs, routes, gates, tokens, out_grad):
    tok, width = tokens.shape
    pairs = expert_pairs.shape[0]
    out = call(
        functools.partial(pack_own_kernel, pairs),
        "pack_own",
        [struct((tok, width + EXTRA))] + [struct((CAP, 2 * width))] * pairs,
        [SMEM] + [VMEM] * 4,
        [VMEM] * (1 + pairs),
        mib=PACK_MIB,
    )(expert_pairs, routes, gates, tokens, out_grad)
    return out[0], list(out[1:])


PACK_MIB = 56


def pack_far_kernel(top, pairs_ref, far_ref, grad_ref, *outs):
    width = grad_ref.shape[1]
    info = far_ref[:, width:].astype(F32).T
    gates = info[top : 2 * top] + info[2 * top : 3 * top] + info[3 * top : 4 * top]
    pick, gate, _ = pick_rows(info[:top], gates, pairs_ref)
    row_gate = jnp.sum(pick * gate, axis=1, keepdims=True)
    pick = pick.astype(BF16)
    put_chunks(dot32(pick, far_ref[:, :width]), [ref.at[:, :width] for ref in outs])
    put_chunks(dot32(pick, grad_ref[...]) * row_gate, [ref.at[:, width:] for ref in outs])


def pack_far(expert_pairs, far, out_grad, top):
    pairs = expert_pairs.shape[0]
    out = call(
        functools.partial(pack_far_kernel, top),
        "pack_far",
        [struct((CAP, 2 * out_grad.shape[1]))] * pairs,
        [SMEM, VMEM, VMEM],
        [VMEM] * pairs,
    )(expert_pairs, far, out_grad)
    return list(out)


def dispatch(chunks, ordered=True):
    pairs = len(chunks)
    split = pairs - pairs // 4 if ordered else pairs
    near = [chunks[0]] + [hop(chunks[d], "expert", d) for d in range(1, split)]
    rest = [hop(after(chunks[d], *near[1:]), "expert", d) for d in range(split, pairs)]
    return near + rest


def load_kernel(*refs):
    copies = [pltpu.make_async_copy(refs[i], refs[3 + i], refs[6].at[i]) for i in range(3)]
    for copy in copies:
        copy.start()
    for copy in copies:
        copy.wait()


def load(weights):
    return call(
        load_kernel,
        "load",
        [struct(w.shape) for w in weights],
        [ANY] * 3,
        [VMEM] * 3,
        [pltpu.SemaphoreType.DMA((3,))],
    )(*weights)


def terms_kernel(count, *refs):
    chunks, (w_gate, w_up, w_down, send_ref, keep_ref) = refs[:count], refs[count:]
    half = send_ref.shape[2]
    width = w_gate.shape[0]
    core = lax.axis_index("dp") % 2
    rows = join([ref.at[:, :width] for ref in chunks])
    cot = join([ref.at[:, width:] for ref in chunks])
    for ref, side in ((send_ref, 1 - core), (keep_ref, core)):
        at = pl.ds(pl.multiple_of(side * half, half), half)
        ref[0] = dot32(rows, w_gate[:, at]).astype(BF16)
        ref[1] = dot32(rows, w_up[:, at]).astype(BF16)
        ref[2] = dot32(cot, w_down[at, :], SECOND).astype(BF16)


def terms(chunks, weights):
    out = struct((3, len(chunks) * CAP, weights[0].shape[1] // 2))
    return call(
        functools.partial(terms_kernel, len(chunks)),
        "terms",
        [out, out],
        [VMEM] * (len(chunks) + 3),
        [VMEM] * 2,
    )(*chunks, *weights)


def add_kernel(spans, *refs):
    *parts, out = refs
    for i in range(out.shape[0]):
        sums = [
            (a[i].astype(F32) + b[i].astype(F32))[lo:hi]
            for a, b, (lo, hi) in zip(parts[::2], parts[1::2], spans)
        ]
        out[i] = jnp.concatenate(sums, axis=0).astype(BF16)


def add(*arrays, spans=None):
    spans = spans or [(0, a.shape[1]) for a in arrays[::2]]
    total = sum(hi - lo for lo, hi in spans)
    shape = arrays[0].shape
    return call(
        functools.partial(add_kernel, spans),
        "add",
        struct((shape[0], total, shape[2])),
        [VMEM] * len(arrays),
        VMEM,
    )(*arrays)


def core_hop(x):
    return hop(x, "dp", 1)


def across(total):
    distance = 2
    parts = [total, hop(total, "dp", distance)]
    while 2 * distance < lax.axis_size("dp"):
        distance *= 2
        total = add(*parts)
        parts = [total, hop(total, "dp", distance)]
    return parts


def middle(gate_pre, up_pre, hidden_grad):
    sig = jax.nn.sigmoid(gate_pre)
    silu = gate_pre * sig
    hidden = silu * up_pre
    up_grad = hidden_grad * silu
    pre_grad = hidden_grad * up_pre * sig * (1.0 + gate_pre * (1.0 - sig))
    return hidden, up_grad, pre_grad


def by_blocks(total, body):
    block = BLOCK if total % BLOCK == 0 else 16

    def step(i, carry):
        body(pl.ds(pl.multiple_of(i * block, block), block))
        return carry

    lax.fori_loop(0, total // block, step, 0)


def sides(mine, other):
    lower = lax.axis_index("dp") % 2 == 0

    def read(side, i, rows):
        a, b = mine[i, rows].astype(F32), other[i, rows].astype(F32)
        return jnp.where(lower, a, b) if side == 0 else jnp.where(lower, b, a)

    return read


def outputs_kernel(pairs, mine, other, w_gate, w_up, w_down, hidden_ref, up_ref, pre_ref, *refs):
    chunks, ends = refs[:pairs], refs[pairs]
    total, half = mine.shape[1:]
    width = w_gate.shape[0]
    read = sides(mine, other)

    def block(rows):
        inner = 0.0
        for side in range(2):
            values = [read(side, i, rows) for i in range(3)]
            hidden, up_grad, pre_grad = middle(*values)
            inner += jnp.sum(hidden * values[2], axis=1, keepdims=True)
            at = slice(side * half, (side + 1) * half)
            hidden_ref[rows, at] = hidden.astype(BF16)
            up_ref[rows, at] = up_grad.astype(BF16)
            pre_ref[rows, at] = pre_grad.astype(BF16)
        high = inner.astype(BF16).astype(F32)
        lane = lax.broadcasted_iota(jnp.int32, (inner.shape[0], EXTRA), 1)
        ends[rows] = jnp.where(lane == 0, high, jnp.where(lane == 1, inner - high, 0.0))

    by_blocks(total, block)
    put_chunks(ends[...], [ref.at[:, 2 * width :] for ref in chunks])
    out = dot32(hidden_ref[...], w_down[...])
    put_chunks(out, [ref.at[:, :width] for ref in chunks])
    out = dot32(pre_ref[...], w_gate[...], SECOND) + dot32(up_ref[...], w_up[...], SECOND)
    put_chunks(out, [ref.at[:, width : 2 * width] for ref in chunks])


def outputs(mine, other, weights, pairs):
    width, hidden = weights[0].shape
    total = pairs * CAP
    out = call(
        functools.partial(outputs_kernel, pairs),
        "outputs",
        [struct((total, hidden))] * 3 + [struct((CAP, 2 * width + EXTRA))] * pairs,
        [VMEM] * 5,
        [VMEM] * (3 + pairs),
        [pltpu.VMEM((total, EXTRA), F32)],
    )(mine, other, *weights)
    return out[:3], list(out[3:])


def combine_kernel(pairs, pairs_ref, routes_ref, gates_ref, *refs):
    chunks = refs[:pairs]
    out_ref, grad_ref, value_ref, back = refs[pairs:]
    tok, width = out_ref.shape
    top = routes_ref.shape[0]
    gates = gates_ref[...]
    pick, gate, hits = pick_rows(routes_ref[...].astype(F32), gates, pairs_ref)
    back[...] = join(chunks)
    scaled = pick * gate
    high = scaled.astype(BF16).astype(F32)
    both = jnp.concatenate([high, scaled - high], axis=1).astype(BF16)
    out = dot32(both, back[:, :width], FIRST)
    out_ref[...] = (out[:tok] + out[tok:]).astype(BF16)
    grad_ref[...] = dot32(pick.astype(BF16), back[:, width : 2 * width], FIRST).astype(BF16)
    ends = back[:, 2 * width :].astype(F32)
    inner = ends[:, 0:1] + ends[:, 1:2]
    values = [jnp.sum(jnp.where(hit, pick * inner, 0.0), axis=0, keepdims=True) for hit in hits]
    value_ref[...] = jnp.concatenate(values, axis=0) / gates


def combine(expert_pairs, routes, gates, chunks, width):
    top, tok = routes.shape
    pairs = len(chunks)
    return call(
        functools.partial(combine_kernel, pairs),
        "combine",
        [struct((tok, width)), struct((tok, width)), struct((top, tok), F32)],
        [SMEM] + [VMEM] * (2 + pairs),
        [VMEM] * 3,
        [pltpu.VMEM((pairs * CAP, chunks[0].shape[1]), BF16)],
    )(expert_pairs, routes, gates, *chunks)


def turn_kernel(count, *refs):
    turned, cot = refs[count:]
    width = cot.shape[1]
    turned[...] = join([ref.at[:, :width] for ref in refs[:count]]).T
    cot[...] = join([ref.at[:, width:] for ref in refs[:count]])


def turn(chunks):
    total, width = len(chunks) * CAP, chunks[0].shape[1] // 2
    return call(
        functools.partial(turn_kernel, len(chunks)),
        "turn",
        [struct((width, total)), struct((total, width))],
        [VMEM] * len(chunks),
        [VMEM] * 2,
    )(*chunks)


def column_step(*widths):
    step = 256
    while any(w % step for w in widths):
        step //= 2
    return step


def grad_shapes(width, units):
    return [struct(shape) for shape in ((width, units), (width, units), (units, width))]


def own_grads_kernel(step, turned, cot, pre_grad, up_grad, hidden, gate_out, up_out, down_out):
    for left, right, out in (
        (turned[...], pre_grad, gate_out),
        (turned[...], up_grad, up_out),
        (hidden[...].T, cot, down_out),
    ):
        for j in range(out.shape[1] // step):
            at = slice(j * step, (j + 1) * step)
            out[:, at] = dot32(left, right[:, at]).astype(BF16)


def own_grads(turned, cot, pre_grad, up_grad, hidden):
    width, units = turned.shape[0], hidden.shape[1]
    return call(
        functools.partial(own_grads_kernel, column_step(units, width)),
        "own_grads",
        grad_shapes(width, units),
        [VMEM] * 5,
        [VMEM] * 3,
    )(turned, cot, pre_grad, up_grad, hidden)


def grads_kernel(step, mine, other, turned, cot, *refs):
    partial, outs, held, buffers, sems = refs[:3], refs[3:6], refs[6], refs[7:10], refs[10]
    total, half = mine.shape[1:]
    read = sides(mine, other)

    def block(rows):
        for side in range(2):
            far_hidden, up, pre = middle(*(read(side, i, rows) for i in range(3)))
            at = slice(side * half, (side + 1) * half)
            for i, part in enumerate((pre, up, far_hidden)):
                held[i, rows, at] = part.astype(BF16)

    by_blocks(total, block)
    copies = []
    for i, right in enumerate((held.at[0], held.at[1], cot)):
        left = held[2].T if i == 2 else turned[...]
        for j in range(outs[i].shape[1] // step):
            at = slice(j * step, (j + 1) * step)
            part = dot32(left, right[:, at]) + partial[i][:, at].astype(F32)
            buffers[i][:, at] = part.astype(BF16)
            copy = pltpu.make_async_copy(buffers[i].at[:, at], outs[i].at[:, at], sems.at[len(copies)])
            copy.start()
            copies.append(copy)
    for copy in copies:
        copy.wait()


def grads(mine, other, turned, cot, partial):
    width, total = turned.shape
    units = partial[0].shape[1]
    step = column_step(units, width)
    shapes = grad_shapes(width, units)
    return call(
        functools.partial(grads_kernel, step),
        "grads",
        shapes,
        [VMEM] * 7,
        [ANY] * 3,
        [pltpu.VMEM((3, total, units), BF16)]
        + [pltpu.VMEM(shape.shape, BF16) for shape in shapes]
        + [pltpu.SemaphoreType.DMA((2 * units // step + width // step,))],
        mib=24,
    )(mine, other, turned, cot, *partial)


def shards(
    tokens, out_grad, gate_values, route_lists, expert_pairs, gate_weight, up_weight, down_weight
):
    top = route_lists.shape[1]
    width = tokens.shape[1]
    pairs = lax.axis_size("expert") // 2
    routes, gates = route_lists.T, gate_values.T

    far, chunks = pack_own(expert_pairs, routes, gates, tokens, out_grad)
    weights = load([after(gate_weight[0], far), up_weight[0], down_weight[0]])
    far = hop(far, "expert", pairs)
    far_grad = hop(after(out_grad, far), "expert", pairs)
    chunks = dispatch(chunks)

    send, keep = terms(chunks[:1], weights)
    sums_a = across(add(keep, core_hop(send)))

    far_chunks = pack_far(expert_pairs, far, after(far_grad, sums_a[1]), top)
    chunks[1] = after(chunks[1], far_chunks[0])
    send, keep = terms(chunks[1:], weights)
    far_chunks = dispatch(far_chunks)
    sums_b = across(add(keep, core_hop(send)))

    far_chunks[1] = after(far_chunks[1], sums_b[1])
    mine = add(*sums_a, *sums_b)
    other = core_hop(mine)
    send, keep = terms(far_chunks, weights)
    got = core_hop(send)
    (hidden, up_grad, pre_grad), sent = outputs(after(mine, send), other, weights, pairs)
    far_sums = across(add(keep, after(got, sent[0])))
    arrived = dispatch(sent, False)

    turned, cot = turn([after(chunks[0], far_sums[0])] + chunks[1:])
    partial = own_grads(turned, cot, pre_grad, up_grad, hidden)
    turned, cot = turn([after(far_chunks[0], partial[0])] + far_chunks[1:])

    far_sums[1] = after(far_sums[1], turned, *arrived[1:])
    mine = add(*far_sums)
    other = core_hop(mine)
    layer_output, token_grad, values = combine(
        expert_pairs, routes, gates, [after(arrived[0], mine)] + arrived[1:], width
    )
    grad_gate, grad_up, grad_down = grads(mine, after(other, token_grad), turned, cot, partial)
    return layer_output, token_grad, values.T, grad_gate[None], grad_up[None], grad_down[None]


def solution(mesh):
    row = P("expert", "dp")
    small = P("expert", None)
    tall = P("expert", "dp", None)
    wide = P("expert", None, "dp")
    return jax.shard_map(
        shards,
        mesh=mesh,
        in_specs=(row, row, small, small, P(), tall, tall, wide),
        out_specs=(row, row, small, tall, tall, wide),
        check_vma=False,
    )
```

```python
import functools

import jax
import jax.numpy as jnp
from jax import lax
from jax.experimental import pallas as pl
from jax.experimental.pallas import tpu as pltpu
from jax.sharding import PartitionSpec as P

HALF = 36
CAP = 2 * HALF
EXTRA = 128
BLOCK = 144
FIRST = (((0,), (0,)), ((), ()))
SECOND = (((1,), (1,)), ((), ()))
PLAIN = (((1,), (0,)), ((), ()))
F32 = jnp.float32
BF16 = jnp.bfloat16

VMEM = pl.BlockSpec(memory_space=pltpu.VMEM)
SMEM = pl.BlockSpec(memory_space=pltpu.SMEM)
ANY = pl.BlockSpec(memory_space=pl.ANY)


def hop(x, axis, distance):
    return lax.ppermute(x, axis, [(i, i ^ distance) for i in range(lax.axis_size(axis))])


def after(x, *first):
    return lax.optimization_barrier((x, *first))[0]


def dot32(a, b, dims=PLAIN):
    return lax.dot_general(a, b, dims, preferred_element_type=F32)


def struct(shape, dtype=BF16):
    return jax.ShapeDtypeStruct(shape, dtype)


def call(kernel, name, out_shape, in_specs, out_specs, scratch=(), mib=20):
    return pl.pallas_call(
        kernel,
        out_shape=out_shape,
        in_specs=in_specs,
        out_specs=out_specs,
        scratch_shapes=scratch,
        compiler_params=pltpu.CompilerParams(vmem_limit_bytes=mib * 2**20),
        cost_estimate=pl.CostEstimate(flops=1024, bytes_accessed=1 << 19, transcendentals=0),
        name=name,
    )


def row_slots(pairs_ref):
    pairs = pairs_ref.shape[0]
    low = lax.axis_index("expert") % pairs
    at = lax.broadcasted_iota(jnp.int32, (pairs * CAP, 1), 0)
    name = jnp.full(at.shape, pairs_ref[low], jnp.int32)
    place = at
    for d in range(1, pairs):
        later = at >= d * CAP
        name = jnp.where(later, pairs_ref[low ^ d], name)
        place = jnp.where(later, at - d * CAP, place)
    return name.astype(F32), place.astype(F32)


def pick_rows(routes, gates, pairs_ref):
    top, tok = routes.shape
    name, place = row_slots(pairs_ref)
    gate = jnp.zeros((name.shape[0], tok), F32)
    named = jnp.zeros((name.shape[0], tok), F32)
    hits = [routes[k : k + 1] == name for k in range(top)]
    for k in range(top):
        named = jnp.where(hits[k], 1.0, named)
        gate = jnp.where(hits[k], gates[k : k + 1], gate)
    earlier = (
        lax.broadcasted_iota(jnp.int32, (tok, tok), 0) < lax.broadcasted_iota(jnp.int32, (tok, tok), 1)
    )
    before = dot32(named.astype(BF16), jnp.where(earlier, 1.0, 0.0).astype(BF16))
    return jnp.where(before == place, named, 0.0), gate, hits


def put_chunks(rows, refs):
    for d, ref in enumerate(refs):
        ref[...] = rows[d * CAP : (d + 1) * CAP].astype(BF16)


def join(refs):
    return jnp.concatenate([r[...].astype(F32) for r in refs], axis=0).astype(BF16)


def pack_own_kernel(pairs, pairs_ref, routes_ref, gates_ref, tok_ref, grad_ref, far_ref, *outs):
    top, tok = routes_ref.shape
    width = tok_ref.shape[1]
    routes = routes_ref[...].astype(F32)
    gates = gates_ref[...]
    far_ref[:, :width] = tok_ref[...]
    high = gates.astype(BF16).astype(F32)
    mid = (gates - high).astype(BF16).astype(F32)
    filler = jnp.zeros((EXTRA - 4 * top, tok), F32)
    info = jnp.concatenate([routes, high, mid, gates - high - mid, filler], axis=0)
    far_ref[:, width:] = info.T.astype(BF16)
    pick, gate, _ = pick_rows(routes, gates, pairs_ref)
    row_gate = jnp.sum(pick * gate, axis=1, keepdims=True)
    pick = pick.astype(BF16)
    put_chunks(dot32(pick, tok_ref[...]), [ref.at[:, :width] for ref in outs])
    put_chunks(dot32(pick, grad_ref[...]) * row_gate, [ref.at[:, width:] for ref in outs])


def pack_own(expert_pairs, routes, gates, tokens, out_grad):
    tok, width = tokens.shape
    pairs = expert_pairs.shape[0]
    out = call(
        functools.partial(pack_own_kernel, pairs),
        "pack_own",
        [struct((tok, width + EXTRA))] + [struct((CAP, 2 * width))] * pairs,
        [SMEM] + [VMEM] * 4,
        [VMEM] * (1 + pairs),
        mib=PACK_MIB,
    )(expert_pairs, routes, gates, tokens, out_grad)
    return out[0], list(out[1:])


PACK_MIB = 56


def pack_far_kernel(top, pairs_ref, far_ref, grad_ref, *outs):
    width = grad_ref.shape[1]
    info = far_ref[:, width:].astype(F32).T
    gates = info[top : 2 * top] + info[2 * top : 3 * top] + info[3 * top : 4 * top]
    pick, gate, _ = pick_rows(info[:top], gates, pairs_ref)
    row_gate = jnp.sum(pick * gate, axis=1, keepdims=True)
    pick = pick.astype(BF16)
    put_chunks(dot32(pick, far_ref[:, :width]), [ref.at[:, :width] for ref in outs])
    put_chunks(dot32(pick, grad_ref[...]) * row_gate, [ref.at[:, width:] for ref in outs])


def pack_far(expert_pairs, far, out_grad, top):
    pairs = expert_pairs.shape[0]
    out = call(
        functools.partial(pack_far_kernel, top),
        "pack_far",
        [struct((CAP, 2 * out_grad.shape[1]))] * pairs,
        [SMEM, VMEM, VMEM],
        [VMEM] * pairs,
    )(expert_pairs, far, out_grad)
    return list(out)


def dispatch(chunks, ordered=True):
    pairs = len(chunks)
    split = pairs - pairs // 4 if ordered else pairs
    near = [chunks[0]] + [hop(chunks[d], "expert", d) for d in range(1, split)]
    rest = [hop(after(chunks[d], *near[1:]), "expert", d) for d in range(split, pairs)]
    return near + rest


def load_kernel(*refs):
    copies = [pltpu.make_async_copy(refs[i], refs[3 + i], refs[6].at[i]) for i in range(3)]
    for copy in copies:
        copy.start()
    for copy in copies:
        copy.wait()


def load(weights):
    return call(
        load_kernel,
        "load",
        [struct(w.shape) for w in weights],
        [ANY] * 3,
        [VMEM] * 3,
        [pltpu.SemaphoreType.DMA((3,))],
    )(*weights)


def terms_kernel(count, *refs):
    chunks, (w_gate, w_up, w_down, send_ref, keep_ref) = refs[:count], refs[count:]
    half = send_ref.shape[2]
    width = w_gate.shape[0]
    core = lax.axis_index("dp") % 2
    rows = join([ref.at[:, :width] for ref in chunks])
    cot = join([ref.at[:, width:] for ref in chunks])
    for ref, side in ((send_ref, 1 - core), (keep_ref, core)):
        at = pl.ds(pl.multiple_of(side * half, half), half)
        ref[0] = dot32(rows, w_gate[:, at]).astype(BF16)
        ref[1] = dot32(rows, w_up[:, at]).astype(BF16)
        ref[2] = dot32(cot, w_down[at, :], SECOND).astype(BF16)


def terms(chunks, weights):
    out = struct((3, len(chunks) * CAP, weights[0].shape[1] // 2))
    return call(
        functools.partial(terms_kernel, len(chunks)),
        "terms",
        [out, out],
        [VMEM] * (len(chunks) + 3),
        [VMEM] * 2,
    )(*chunks, *weights)


def add_kernel(spans, *refs):
    *parts, out = refs
    for i in range(out.shape[0]):
        sums = [
            (a[i].astype(F32) + b[i].astype(F32))[lo:hi]
            for a, b, (lo, hi) in zip(parts[::2], parts[1::2], spans)
        ]
        out[i] = jnp.concatenate(sums, axis=0).astype(BF16)


def add(*arrays, spans=None):
    spans = spans or [(0, a.shape[1]) for a in arrays[::2]]
    total = sum(hi - lo for lo, hi in spans)
    shape = arrays[0].shape
    return call(
        functools.partial(add_kernel, spans),
        "add",
        struct((shape[0], total, shape[2])),
        [VMEM] * len(arrays),
        VMEM,
    )(*arrays)


def core_hop(x):
    return hop(x, "dp", 1)


def across(total):
    distance = 2
    parts = [total, hop(total, "dp", distance)]
    while 2 * distance < lax.axis_size("dp"):
        distance *= 2
        total = add(*parts)
        parts = [total, hop(total, "dp", distance)]
    return parts


def middle(gate_pre, up_pre, hidden_grad):
    sig = jax.nn.sigmoid(gate_pre)
    silu = gate_pre * sig
    hidden = silu * up_pre
    up_grad = hidden_grad * silu
    pre_grad = hidden_grad * up_pre * sig * (1.0 + gate_pre * (1.0 - sig))
    return hidden, up_grad, pre_grad


def by_blocks(total, body):
    block = BLOCK if total % BLOCK == 0 else 16

    def step(i, carry):
        body(pl.ds(pl.multiple_of(i * block, block), block))
        return carry

    lax.fori_loop(0, total // block, step, 0)


def sides(mine, other):
    lower = lax.axis_index("dp") % 2 == 0

    def read(side, i, rows):
        a, b = mine[i, rows].astype(F32), other[i, rows].astype(F32)
        return jnp.where(lower, a, b) if side == 0 else jnp.where(lower, b, a)

    return read


def outputs_kernel(pairs, mine, other, w_gate, w_up, w_down, hidden_ref, up_ref, pre_ref, *refs):
    chunks, ends = refs[:pairs], refs[pairs]
    total, half = mine.shape[1:]
    width = w_gate.shape[0]
    read = sides(mine, other)

    def block(rows):
        inner = 0.0
        for side in range(2):
            values = [read(side, i, rows) for i in range(3)]
            hidden, up_grad, pre_grad = middle(*values)
            inner += jnp.sum(hidden * values[2], axis=1, keepdims=True)
            at = slice(side * half, (side + 1) * half)
            hidden_ref[rows, at] = hidden.astype(BF16)
            up_ref[rows, at] = up_grad.astype(BF16)
            pre_ref[rows, at] = pre_grad.astype(BF16)
        high = inner.astype(BF16).astype(F32)
        lane = lax.broadcasted_iota(jnp.int32, (inner.shape[0], EXTRA), 1)
        ends[rows] = jnp.where(lane == 0, high, jnp.where(lane == 1, inner - high, 0.0))

    by_blocks(total, block)
    put_chunks(ends[...], [ref.at[:, 2 * width :] for ref in chunks])
    out = dot32(hidden_ref[...], w_down[...])
    put_chunks(out, [ref.at[:, :width] for ref in chunks])
    out = dot32(pre_ref[...], w_gate[...], SECOND) + dot32(up_ref[...], w_up[...], SECOND)
    put_chunks(out, [ref.at[:, width : 2 * width] for ref in chunks])


def outputs(mine, other, weights, pairs):
    width, hidden = weights[0].shape
    total = pairs * CAP
    out = call(
        functools.partial(outputs_kernel, pairs),
        "outputs",
        [struct((total, hidden))] * 3 + [struct((CAP, 2 * width + EXTRA))] * pairs,
        [VMEM] * 5,
        [VMEM] * (3 + pairs),
        [pltpu.VMEM((total, EXTRA), F32)],
    )(mine, other, *weights)
    return out[:3], list(out[3:])


def combine_kernel(pairs, pairs_ref, routes_ref, gates_ref, *refs):
    chunks = refs[:pairs]
    out_ref, grad_ref, value_ref, back = refs[pairs:]
    tok, width = out_ref.shape
    top = routes_ref.shape[0]
    gates = gates_ref[...]
    pick, gate, hits = pick_rows(routes_ref[...].astype(F32), gates, pairs_ref)
    back[...] = join(chunks)
    scaled = pick * gate
    high = scaled.astype(BF16).astype(F32)
    both = jnp.concatenate([high, scaled - high], axis=1).astype(BF16)
    out = dot32(both, back[:, :width], FIRST)
    out_ref[...] = (out[:tok] + out[tok:]).astype(BF16)
    grad_ref[...] = dot32(pick.astype(BF16), back[:, width : 2 * width], FIRST).astype(BF16)
    ends = back[:, 2 * width :].astype(F32)
    inner = ends[:, 0:1] + ends[:, 1:2]
    values = [jnp.sum(jnp.where(hit, pick * inner, 0.0), axis=0, keepdims=True) for hit in hits]
    value_ref[...] = jnp.concatenate(values, axis=0) / gates


def combine(expert_pairs, routes, gates, chunks, width):
    top, tok = routes.shape
    pairs = len(chunks)
    return call(
        functools.partial(combine_kernel, pairs),
        "combine",
        [struct((tok, width)), struct((tok, width)), struct((top, tok), F32)],
        [SMEM] + [VMEM] * (2 + pairs),
        [VMEM] * 3,
        [pltpu.VMEM((pairs * CAP, chunks[0].shape[1]), BF16)],
    )(expert_pairs, routes, gates, *chunks)


def turn_kernel(count, *refs):
    turned, cot = refs[count:]
    width = cot.shape[1]
    turned[...] = join([ref.at[:, :width] for ref in refs[:count]]).T
    cot[...] = join([ref.at[:, width:] for ref in refs[:count]])


def turn(chunks):
    total, width = len(chunks) * CAP, chunks[0].shape[1] // 2
    return call(
        functools.partial(turn_kernel, len(chunks)),
        "turn",
        [struct((width, total)), struct((total, width))],
        [VMEM] * len(chunks),
        [VMEM] * 2,
    )(*chunks)


def column_step(*widths):
    step = 256
    while any(w % step for w in widths):
        step //= 2
    return step


def grad_shapes(width, units):
    return [struct(shape) for shape in ((width, units), (width, units), (units, width))]


def own_grads_kernel(step, turned, cot, pre_grad, up_grad, hidden, gate_out, up_out, down_out):
    for left, right, out in (
        (turned[...], pre_grad, gate_out),
        (turned[...], up_grad, up_out),
        (hidden[...].T, cot, down_out),
    ):
        for j in range(out.shape[1] // step):
            at = slice(j * step, (j + 1) * step)
            out[:, at] = dot32(left, right[:, at]).astype(BF16)


def own_grads(turned, cot, pre_grad, up_grad, hidden):
    width, units = turned.shape[0], hidden.shape[1]
    return call(
        functools.partial(own_grads_kernel, column_step(units, width)),
        "own_grads",
        grad_shapes(width, units),
        [VMEM] * 5,
        [VMEM] * 3,
    )(turned, cot, pre_grad, up_grad, hidden)


def grads_kernel(step, mine, other, turned, cot, *refs):
    partial, outs, held, buffers, sems = refs[:3], refs[3:6], refs[6], refs[7:10], refs[10]
    total, half = mine.shape[1:]
    read = sides(mine, other)

    def block(rows):
        for side in range(2):
            far_hidden, up, pre = middle(*(read(side, i, rows) for i in range(3)))
            at = slice(side * half, (side + 1) * half)
            for i, part in enumerate((pre, up, far_hidden)):
                held[i, rows, at] = part.astype(BF16)

    by_blocks(total, block)
    copies = []
    for i, right in enumerate((held.at[0], held.at[1], cot)):
        left = held[2].T if i == 2 else turned[...]
        for j in range(outs[i].shape[1] // step):
            at = slice(j * step, (j + 1) * step)
            part = dot32(left, right[:, at]) + partial[i][:, at].astype(F32)
            buffers[i][:, at] = part.astype(BF16)
            copy = pltpu.make_async_copy(buffers[i].at[:, at], outs[i].at[:, at], sems.at[len(copies)])
            copy.start()
            copies.append(copy)
    for copy in copies:
        copy.wait()


def grads(mine, other, turned, cot, partial):
    width, total = turned.shape
    units = partial[0].shape[1]
    step = column_step(units, width)
    shapes = grad_shapes(width, units)
    return call(
        functools.partial(grads_kernel, step),
        "grads",
        shapes,
        [VMEM] * 7,
        [ANY] * 3,
        [pltpu.VMEM((3, total, units), BF16)]
        + [pltpu.VMEM(shape.shape, BF16) for shape in shapes]
        + [pltpu.SemaphoreType.DMA((2 * units // step + width // step,))],
        mib=24,
    )(mine, other, turned, cot, *partial)


def shards(
    tokens, out_grad, gate_values, route_lists, expert_pairs, gate_weight, up_weight, down_weight
):
    top = route_lists.shape[1]
    width = tokens.shape[1]
    pairs = lax.axis_size("expert") // 2
    routes, gates = route_lists.T, gate_values.T

    far, chunks = pack_own(expert_pairs, routes, gates, tokens, out_grad)
    weights = load([after(gate_weight[0], far), up_weight[0], down_weight[0]])
    far = hop(far, "expert", pairs)
    far_grad = hop(after(out_grad, far), "expert", pairs)
    chunks = dispatch(chunks)

    send, keep = terms(chunks[:1], weights)
    sums_a = across(add(keep, core_hop(send)))

    far_chunks = pack_far(expert_pairs, far, after(far_grad, sums_a[1]), top)
    chunks[1] = after(chunks[1], far_chunks[0])
    send, keep = terms(chunks[1:], weights)
    far_chunks = dispatch(far_chunks)
    sums_b = across(add(keep, core_hop(send)))

    far_chunks[1] = after(far_chunks[1], sums_b[1])
    mine = add(*sums_a, *sums_b)
    other = core_hop(mine)
    send, keep = terms(far_chunks, weights)
    got = core_hop(send)
    (hidden, up_grad, pre_grad), sent = outputs(after(mine, send), other, weights, pairs)
    far_sums = across(add(keep, after(got, sent[0])))
    arrived = dispatch(sent, False)

    turned, cot = turn([after(chunks[0], far_sums[0])] + chunks[1:])
    partial = own_grads(turned, cot, pre_grad, up_grad, hidden)
    turned, cot = turn([after(far_chunks[0], partial[0])] + far_chunks[1:])

    far_sums[1] = after(far_sums[1], turned, *arrived[1:])
    mine = add(*far_sums)
    other = core_hop(mine)
    layer_output, token_grad, values = combine(
        expert_pairs, routes, gates, [after(arrived[0], mine)] + arrived[1:], width
    )
    grad_gate, grad_up, grad_down = grads(mine, after(other, token_grad), turned, cot, partial)
    return layer_output, token_grad, values.T, grad_gate[None], grad_up[None], grad_down[None]


def solution(mesh):
    row = P("expert", "dp")
    small = P("expert", None)
    tall = P("expert", "dp", None)
    wide = P("expert", None, "dp")
    return jax.shard_map(
        shards,
        mesh=mesh,
        in_specs=(row, row, small, small, P(), tall, tall, wide),
        out_specs=(row, row, small, tall, tall, wide),
        check_vma=False,
    )
```
